256 devices in a mesh: seq: 32 (over y_hi, z, core), ch: 8 (over y_lo, x).
Axes of the slice: x: 4, y: 4 (y_hi: 2, y_lo: 2; y = y_hi * 2 + y_lo), z: 8, core: 2. Of those that a mesh axis runs over, the one named last changes fastest.
Arguments:
- cotangent: bfloat16 [4096, 4096], P('seq', 'ch'), may hold values from -6 to 6
- keep_mask: int32 [4096, 4096], P('seq', 'ch'), may hold values 0 or 1
- gate_out: bfloat16 [4096, 4096], P('seq', 'ch'), may hold values from -6 to 6
- gate_in: bfloat16 [4096, 4096], P('seq', 'ch'), may hold values from -6 to 6
- value_in: bfloat16 [4096, 4096], P('seq', 'ch'), may hold values from -6 to 6
- filter_taps: float32 [4096, 4096], P('seq', 'ch'), may hold values from -3 to 3
- out_weight: bfloat16 [4096, 4096], P('seq', 'ch'), may hold values from -0.09375 to 0.09375
Outputs:
- grad_gate_out: bfloat16 [4096, 4096], P('seq', 'ch')
- grad_gate_in: bfloat16 [4096, 4096], P('seq', 'ch')
- grad_value: bfloat16 [4096, 4096], P('seq', 'ch')
- grad_filter: float32 [4096, 4096], P('seq', 'ch')
- grad_weight: float32 [4096, 4096], P('seq', 'ch')
The draws below stay inside these ranges and needn't reach their ends.
All inputs are finite; a program needn't handle non-finite values. No bound on the sum of `keep_mask` on one device may be relied on, other than what follows from the above.
Results may differ from the reference program's by a relative error of at most 0.023.
Values may be sent and summed in bfloat16 or wider, within the bound.
No kernel may reach another device: no remote copies, remote signals or barrier semaphores. Data moves between devices by JAX's collectives and lax.ppermute only.
A program may use at most 64 MiB of HBM per device.

```python
import math
import jax
import jax.numpy as jnp
from jax import lax

D = 4096
TOKEN_COUNT = 4096


def draw_filter_taps(key, part):
    key = jax.random.fold_in(key, 7)
    random_subkeys = jax.random.split(key, 6)
    slow_rate = jax.random.uniform(random_subkeys[1], (D,), minval=math.log(0.3 / TOKEN_COUNT), maxval=math.log(2.0 / TOKEN_COUNT))
    fast_rate = jax.random.uniform(random_subkeys[2], (D,), minval=math.log(2.0 / TOKEN_COUNT), maxval=math.log(1.0 / 20.0))
    channel_kind = jax.random.randint(random_subkeys[0], (D,), 0, 2)
    decay_rate = jnp.exp(jnp.where(channel_kind == 1, fast_rate, slow_rate))
    rough_part = jnp.clip(jax.random.normal(random_subkeys[5], (TOKEN_COUNT, D)), -4.0, 4.0)
    token_positions = jnp.arange(TOKEN_COUNT).astype(jnp.float32)[:, None]
    decay_envelope = jnp.exp(-token_positions * decay_rate[None, :]) * jnp.sqrt(1.0 - jnp.exp(-2.0 * decay_rate))[None, :]
    pulse_location = jax.random.randint(random_subkeys[3], (4,), 0, TOKEN_COUNT)
    pulse_keep_mask = jax.random.uniform(random_subkeys[4], (4,), minval=0.5, maxval=0.8)
    for pulse_signal in range(4):
        decay_envelope = decay_envelope * jnp.where(token_positions >= pulse_location[pulse_signal].astype(jnp.float32), pulse_keep_mask[pulse_signal], 1.0)
    return (decay_envelope * rough_part).astype(jnp.float32)


def touch_ends(result, own_key, least, top_value):
    longest = result.shape.index(max(result.shape))
    spots = []
    for shift in (0, 1):
        where = [jax.random.randint(jax.random.fold_in(own_key, axis), (), 0, length) for axis, length in enumerate(result.shape)]
        where[longest] = (where[longest] + shift) % result.shape[longest]
        spots.append(tuple(where))
    return result.at[spots[0]].set(least).at[spots[1]].set(top_value)


def levels(stream_key, extent, cuts, least, top_value):
    def one(position, shards_of):
        heights = jax.random.uniform(jax.random.fold_in(jax.random.fold_in(stream_key, 6), position), (shards_of,), jnp.float32, least / len(cuts), top_value / len(cuts))
        return jnp.repeat(jnp.exp(heights), extent[position] // shards_of).reshape((-1,) + (1,) * (len(extent) - position - 1))

    level = one(*cuts[0])
    for cut in cuts[1:]:
        level = level * one(*cut)
    return level


def bell_draw(key, dims, deviation, bound, cuts=(), dtype=jnp.bfloat16):
    values = deviation * jax.random.normal(key, dims, jnp.float32)
    if cuts:
        values = values * levels(key, dims, cuts, -0.22, 0.18)
    return jnp.clip(values, -bound, bound).astype(dtype)


def setup_inputs(seed: int = 0) -> dict:
    streams_of = jax.random.split(jax.random.key(seed), 8)
    cotangent = bell_draw(streams_of[0], (TOKEN_COUNT, D), 1.0, 6.0, ((0, 32), (1, 8)))
    keep_mask = touch_ends((jax.random.randint(streams_of[1], (TOKEN_COUNT, D), 0, 10) < 9).astype(jnp.int32), jax.random.fold_in(streams_of[1], 1), 0, 1)
    gate_out = bell_draw(streams_of[2], (TOKEN_COUNT, D), 1.0, 6.0, ((0, 32), (1, 8)))
    gate_in = bell_draw(streams_of[3], (TOKEN_COUNT, D), 1.0, 6.0, ((0, 32), (1, 8)))
    value_in = bell_draw(streams_of[4], (TOKEN_COUNT, D), 1.0, 6.0, ((0, 32), (1, 8)))
    filter_taps = draw_filter_taps(jax.random.fold_in(streams_of[7], 71), 0)
    out_weight = bell_draw(streams_of[6], (D, D), D ** -0.5, 0.09375, ((0, 32), (1, 8)))
    return {"cotangent": cotangent, "keep_mask": keep_mask, "gate_out": gate_out, "gate_in": gate_in, "value_in": value_in, "filter_taps": filter_taps, "out_weight": out_weight}


keep_prob = 0.9

def spectral(blocks):
    prod_block, taps_block, grad_block = blocks
    size_all = 2 * TOKEN_COUNT
    prod_freq = jnp.fft.rfft(prod_block, n=size_all, axis=0)
    taps_freq = jnp.fft.rfft(taps_block, n=size_all, axis=0)
    grad_freq = jnp.fft.rfft(grad_block, n=size_all, axis=0)
    conv = jnp.fft.irfft(taps_freq * prod_freq, n=size_all, axis=0)[:TOKEN_COUNT]
    back = jnp.fft.irfft(grad_freq * jnp.conj(taps_freq), n=size_all, axis=0)[:TOKEN_COUNT]
    taps_grad = jnp.fft.irfft(grad_freq * jnp.conj(prod_freq), n=size_all, axis=0)[:TOKEN_COUNT]
    return (conv.astype(jnp.bfloat16), back.astype(jnp.bfloat16), (taps_grad / math.sqrt(TOKEN_COUNT)).astype(jnp.float32))

def reference(cotangent, keep_mask, gate_out, gate_in, value_in, filter_taps, out_weight):
    product = (gate_in.astype(jnp.float32) * value_in.astype(jnp.float32)).astype(jnp.bfloat16)
    dropped = (cotangent.astype(jnp.float32) * keep_mask.astype(jnp.float32) / keep_prob).astype(jnp.bfloat16)
    grad_mixed = jnp.dot(dropped, out_weight, preferred_element_type=jnp.float32)
    conv_grad = (grad_mixed * gate_out.astype(jnp.float32)).astype(jnp.bfloat16)
    block_width = min(D, 256)
    block_count = D // block_width

    def split_blocks(array):
        return array.reshape(TOKEN_COUNT, block_count, block_width).transpose(1, 0, 2)

    def join_blocks(array):
        return array.transpose(1, 0, 2).reshape(TOKEN_COUNT, D)
    conv_b, back_b, taps_b = lax.map(spectral, (split_blocks(product.astype(jnp.float32)), split_blocks(filter_taps.astype(jnp.float32)), split_blocks(conv_grad.astype(jnp.float32))))
    conv = join_blocks(conv_b)
    back = join_blocks(back_b)
    grad_filter = join_blocks(taps_b)
    mixed_act = (gate_out.astype(jnp.float32) * conv.astype(jnp.float32)).astype(jnp.bfloat16)
    grad_weight = jnp.dot(dropped.T, mixed_act, preferred_element_type=jnp.float32) / math.sqrt(TOKEN_COUNT)
    grad_gate_out = (grad_mixed * conv.astype(jnp.float32)).astype(jnp.bfloat16)
    grad_gate_in = (back.astype(jnp.float32) * value_in.astype(jnp.float32)).astype(jnp.bfloat16)
    grad_value = (back.astype(jnp.float32) * gate_in.astype(jnp.float32)).astype(jnp.bfloat16)
    return (grad_gate_out, grad_gate_in, grad_value, grad_filter, grad_weight)
```

```python
import math
import jax, jax.numpy as jnp, numpy as np, ml_dtypes
from jax import lax
from jax.sharding import Mesh, PartitionSpec as P
from jax.experimental import pallas as pl
from jax.experimental.pallas import tpu as pltpu

BF = jnp.bfloat16
F32 = jnp.float32
BLK = 128
NBLK = 32
GRP = 16
FRQ = 40
LEN = 2 * BLK * NBLK


def split_np(table):
    hi = table.astype(ml_dtypes.bfloat16)
    lo = (table - hi.astype(np.float64)).astype(ml_dtypes.bfloat16)
    return hi, lo


def tables():
    f1 = np.arange(FRQ)[:, None]
    live = (f1 <= NBLK).astype(np.float64)
    k = np.arange(NBLK)[None, :]
    ang = 2 * np.pi * ((f1 * k) % (2 * NBLK)) / (2 * NBLK)
    first = np.concatenate([np.cos(ang) * live, -np.sin(ang) * live], 0)
    weight = np.where((f1 == 0) | (f1 == NBLK), 1.0, 2.0) * live / LEN
    last = np.concatenate([np.cos(ang) * weight, -np.sin(ang) * weight], 0).T
    s = np.arange(BLK)
    turn = 2 * np.pi * (f1 * s[None, :]) / LEN
    ang2 = 2 * np.pi * ((s[:, None] * s[None, :]) % BLK) / BLK
    c, d = np.cos(ang2), np.sin(ang2)
    fwd = np.block([[c, -d], [d, c]])
    inv = np.block([[c, d], [-d, c]])
    first = np.concatenate(split_np(first), 0)
    last = np.concatenate(split_np(last), 0)
    return (first, np.cos(turn).astype(np.float32), np.sin(turn).astype(np.float32),
            *split_np(fwd), *split_np(inv), last)


def split(x):
    hi = x.astype(BF)
    return hi, (x - hi.astype(F32)).astype(BF)


def dot(a, b):
    return jnp.dot(a, b, preferred_element_type=F32)


def wide_dot(x, hi_tab, lo_tab):
    hi, lo = split(x)
    return dot(hi, hi_tab) + dot(lo, hi_tab) + dot(hi, lo_tab)


def to_freq(src, rows, work, first, cos_t, sin_t, fwd_hi, fwd_lo):
    rows[...] = src.astype(F32).reshape(NBLK * GRP, BLK)
    lanes = jnp.concatenate([rows[pl.ds(g, NBLK, stride=GRP), :] for g in range(GRP)], axis=1).astype(BF)
    both = dot(first, lanes)
    part = both[: 2 * FRQ] + both[2 * FRQ:]
    for g in range(GRP):
        re = part[:FRQ, g * BLK:(g + 1) * BLK]
        im = part[FRQ:, g * BLK:(g + 1) * BLK]
        work[g * FRQ:(g + 1) * FRQ, :BLK] = re * cos_t + im * sin_t
        work[g * FRQ:(g + 1) * FRQ, BLK:] = im * cos_t - re * sin_t
    return wide_dot(work[...], fwd_hi, fwd_lo)


def from_freq(re, im, rows, cos_t, sin_t, inv_hi, inv_lo, last):
    z = wide_dot(jnp.concatenate([re, im], axis=1), inv_hi, inv_lo)
    pieces = []
    for g in range(GRP):
        zr = z[g * FRQ:(g + 1) * FRQ, :BLK]
        zi = z[g * FRQ:(g + 1) * FRQ, BLK:]
        pieces.append(jnp.concatenate([zr * cos_t - zi * sin_t, zr * sin_t + zi * cos_t], axis=0))
    hi, lo = split(jnp.concatenate(pieces, axis=1))
    both = dot(last, hi)
    out = both[:NBLK] + both[NBLK:] + dot(last[:NBLK], lo)
    for g in range(GRP):
        rows[pl.ds(g, NBLK, stride=GRP), :] = out[:, g * BLK:(g + 1) * BLK]
    return rows[...]


def conv_kernel(both, first, cos_t, sin_t, fwd_hi, fwd_lo, inv_hi, inv_lo, last, conv, taps_f, prod_f, rows, work):
    args = (first[...], cos_t[...], sin_t[...], fwd_hi[...], fwd_lo[...])
    taps = to_freq(both[:, :GRP], rows, work, *args)
    taps_f[...] = taps
    prod = to_freq(both[:, GRP:], rows, work, *args)
    prod_f[...] = prod
    tr, ti, pr, pi = taps[:, :BLK], taps[:, BLK:], prod[:, :BLK], prod[:, BLK:]
    out = from_freq(tr * pr - ti * pi, tr * pi + ti * pr, rows, cos_t[...], sin_t[...], inv_hi[...], inv_lo[...], last[...])
    conv[...] = out.astype(BF).reshape(NBLK, GRP, BLK)


def grad_kernel(grad, taps_f, prod_f, first, cos_t, sin_t, fwd_hi, fwd_lo, inv_hi, inv_lo, last, out_ref, rows, work):
    g = to_freq(grad[...], rows, work, first[...], cos_t[...], sin_t[...], fwd_hi[...], fwd_lo[...])
    gr, gi = g[:, :BLK], g[:, BLK:]
    for n, other in enumerate((taps_f, prod_f)):
        r, i = other[:, :BLK], other[:, BLK:]
        out = from_freq(gr * r + gi * i, gi * r - gr * i, rows, cos_t[...], sin_t[...], inv_hi[...], inv_lo[...], last[...])
        if n:
            out = out * (1.0 / math.sqrt(BLK * NBLK))
        out_ref[:, n * GRP:(n + 1) * GRP] = out.astype(BF).reshape(NBLK, GRP, BLK)


def scratch():
    return [pltpu.VMEM((NBLK * GRP, BLK), F32), pltpu.VMEM((GRP * FRQ, 2 * BLK), F32)]


PARAMS = dict(compiler_params=pltpu.CompilerParams(vmem_limit_bytes=32 * 1024 * 1024))


def conv_call(both):
    spec = jax.ShapeDtypeStruct((GRP * FRQ, 2 * BLK), F32)
    return pl.pallas_call(
        conv_kernel,
        out_shape=(jax.ShapeDtypeStruct((NBLK, GRP, BLK), BF), spec, spec),
        scratch_shapes=scratch(), **PARAMS,
    )(both, *tables())


def grad_call(grad, taps_f, prod_f):
    return pl.pallas_call(
        grad_kernel,
        out_shape=jax.ShapeDtypeStruct((NBLK, 2 * GRP, BLK), BF),
        scratch_shapes=scratch(), **PARAMS,
    )(grad, taps_f, prod_f, *tables())


keep_prob = 0.9
SEQ = ("yh", "z", "c")
CH = ("yl", "x")
NZ = 8
NX = 4


def shift_by(axis, size, shift):
    return [(i, (i + shift) % size) for i in range(size)]


def permute(value, axis, size, shift):
    return lax.ppermute(value, axis, shift_by(axis, size, shift))


def f32dot(a, b):
    return jnp.dot(a, b, preferred_element_type=F32)


def to_channels(block):
    return block.T.reshape(NBLK, GRP, BLK)


def body(cotangent, keep_mask, gate_out, gate_in, value_in, filter_taps, out_weight):
    yh, z, c = lax.axis_index("yh"), lax.axis_index("z"), lax.axis_index("c")
    yl, x = lax.axis_index("yl"), lax.axis_index("x")
    scale_back = 1.0 / math.sqrt(BLK * NBLK)
    gate_out32 = gate_out.astype(F32)
    product = (gate_in.astype(F32) * value_in.astype(F32)).astype(BF)
    both = jnp.concatenate([to_channels(filter_taps.astype(BF)), to_channels(product)], axis=1)
    both = lax.all_to_all(both, SEQ, split_axis=0, concat_axis=0, tiled=True)

    weights = [out_weight] + [permute(out_weight, "z", NZ, -s) for s in range(1, NZ)]

    dropped = (cotangent.astype(F32) * keep_mask.astype(F32) / keep_prob).astype(BF)
    chunks = dropped.reshape(BLK, 2, 2, BLK)
    first, second = chunks[:, :, 0].reshape(BLK, 2 * BLK), chunks[:, :, 1].reshape(BLK, 2 * BLK)
    mine = jnp.where(c == 0, first, second)
    theirs = jnp.where(c == 0, second, first)
    pair = jnp.concatenate([mine, permute(theirs, "c", 2, 1)], axis=0)
    near = lax.ppermute(pair, ("yh", "yl"), [(0, 0), (2, 1), (1, 2), (3, 3)])
    far = lax.ppermute(pair, ("yh", "yl"), [(2, 0), (0, 1), (3, 2), (1, 3)])
    quad = jnp.concatenate([near, far], axis=0)
    pieces = [quad] + [permute(quad, "x", NX, -s) for s in range(1, NX)]
    columns = jnp.concatenate(pieces, axis=1)

    stacked = jnp.concatenate(weights, axis=0)
    start = (2 * x - z) % NZ * BLK
    doubled = jnp.concatenate([stacked, stacked], axis=0)
    aligned = lax.dynamic_slice_in_dim(doubled, start, NZ * BLK, axis=0)
    partial = f32dot(columns, aligned)

    partial = partial.reshape(2, 2, BLK, 4 * BLK)
    kept, sent = partial[:, 0], partial[:, 1]
    halves = kept + permute(sent.astype(BF), "c", 2, 1).astype(F32)
    swap = yh != yl
    own = jnp.where(swap, halves[1], halves[0])
    away = jnp.where(swap, halves[0], halves[1])
    grad_mixed = own + permute(away.astype(BF), "yh", 2, 1).astype(F32)

    conv_grad = (grad_mixed * gate_out32).astype(BF)

    conv_f, taps_f, prod_f = conv_call(both)
    conv = lax.all_to_all(conv_f, SEQ, split_axis=0, concat_axis=0, tiled=True).reshape(4 * BLK, BLK).T

    mixed_act = (gate_out32 * conv.astype(F32)).astype(BF)
    mixed_pair = jnp.concatenate([mixed_act, permute(mixed_act, "c", 2, 1)], axis=0)
    other_pair = permute(mixed_pair, "yh", 2, 1)
    mixed = jnp.concatenate([jnp.where(swap, other_pair, mixed_pair), jnp.where(swap, mixed_pair, other_pair)], axis=0)
    grad_w = lax.dot_general(columns, mixed, (((0,), (0,)), ((), ())), preferred_element_type=F32).astype(BF)
    grad_w = jnp.concatenate([grad_w, grad_w], axis=0)
    start_w = (z - 2 * x) % NZ * BLK
    grad_w = lax.dynamic_slice_in_dim(grad_w, start_w, NZ * BLK, axis=0).reshape(NZ, BLK, 4 * BLK)
    total = grad_w[0].astype(F32)
    for s in range(1, NZ):
        total = total + permute(grad_w[s], "z", NZ, s).astype(F32)
    grad_weight = total * scale_back

    grad_chan = lax.all_to_all(to_channels(conv_grad), SEQ, split_axis=0, concat_axis=0, tiled=True)
    outs = grad_call(grad_chan, taps_f, prod_f)
    outs = lax.all_to_all(outs, SEQ, split_axis=0, concat_axis=0, tiled=True)
    back = outs[:, :GRP].reshape(4 * BLK, BLK).T.astype(F32)
    grad_filter = outs[:, GRP:].reshape(4 * BLK, BLK).T.astype(F32)
    grad_gate_out = (grad_mixed * conv.astype(F32)).astype(BF)
    grad_gate_in = (back * value_in.astype(F32)).astype(BF)
    grad_value = (back * gate_in.astype(F32)).astype(BF)
    return (grad_gate_out, grad_gate_in, grad_value, grad_filter, grad_weight)


def solution(mesh):
    fine = Mesh(mesh.devices.reshape(2, NZ, 2, 2, NX), ("yh", "z", "c", "yl", "x"))
    spec = P(SEQ, CH)
    return jax.shard_map(body, mesh=fine, in_specs=(spec,) * 7, out_specs=(spec,) * 5, check_vma=False)
```

```python
import math

import jax
import jax.numpy as jnp
import ml_dtypes
import numpy as np
from jax import lax
from jax.experimental import pallas as pl
from jax.experimental.pallas import tpu as pltpu
from jax.sharding import Mesh, PartitionSpec as P

BF = jnp.bfloat16
F32 = jnp.float32
SDS = jax.ShapeDtypeStruct
keep_prob = 0.9
BLK = 128
NBLK = 32
GRP = 16
FRQ = 40
LEN = 2 * BLK * NBLK
WID = 4 * BLK
TOK = 8 * BLK
NL = 4
ROOT = 1.0 / math.sqrt(BLK * NBLK)
AXES = ("yh", "zl", "zo", "c", "yl", "x")
SEQ = ("yh", "zl", "zo", "c")
CH = ("yl", "x")
OWNED = [(p // 16) * 16 + (p // 2 % 2) * 8 + (p % 2) * 4 + (p // 4 % 4) for p in range(NBLK)]


def split_np(table):
    hi = table.astype(ml_dtypes.bfloat16)
    return hi, (table - hi.astype(np.float64)).astype(ml_dtypes.bfloat16)


def tables():
    f1 = np.arange(FRQ)[:, None]
    live = (f1 <= NBLK).astype(np.float64)
    k = np.arange(NBLK)[None, :]
    ang = 2 * np.pi * ((f1 * k) % (2 * NBLK)) / (2 * NBLK)
    first = np.concatenate([np.cos(ang) * live, -np.sin(ang) * live], 0)
    weight = np.where((f1 == 0) | (f1 == NBLK), 1.0, 2.0) * live / LEN
    last = np.concatenate([np.cos(ang) * weight, -np.sin(ang) * weight], 0).T
    s = np.arange(BLK)
    turns = 2 * np.pi * (f1 * s[None, :]) / LEN
    ang2 = 2 * np.pi * ((s[:, None] * s[None, :]) % BLK) / BLK
    c, d = np.cos(ang2), np.sin(ang2)
    fwd = np.block([[c, -d], [d, c]])
    inv = np.block([[c, d], [-d, c]])
    parts = [*split_np(fwd), *split_np(inv), *split_np(first), *split_np(last)]
    flat = np.zeros((sum(p.shape[0] for p in parts), 2 * BLK), ml_dtypes.bfloat16)
    at = 0
    for p in parts:
        flat[at:at + p.shape[0], :p.shape[1]] = p
        at += p.shape[0]
    return flat, np.concatenate([np.cos(turns), np.sin(turns)], 0).astype(np.float32)


def dot(a, b):
    return jnp.dot(a, b, preferred_element_type=F32)


def split(x):
    hi = x.astype(BF)
    return hi, (x - hi.astype(F32)).astype(BF)


def wide_dot(x, tab, at):
    hi, lo = split(x)
    hi_tab, lo_tab = tab[at:at + 2 * BLK, :], tab[at + 2 * BLK:at + 4 * BLK, :]
    return dot(hi, hi_tab) + dot(lo, hi_tab) + dot(hi, lo_tab)


def to_freq(rows, work, tab, trig):
    cos_t, sin_t = trig[:FRQ, :], trig[FRQ:, :]
    lanes = jnp.concatenate([rows[pl.ds(g, NBLK, stride=GRP), :] for g in range(GRP)], axis=1).astype(BF)
    both = dot(tab[8 * BLK:8 * BLK + 4 * FRQ, :NBLK], lanes)
    part = both[:2 * FRQ] + both[2 * FRQ:]
    for g in range(GRP):
        re = part[:FRQ, g * BLK:(g + 1) * BLK]
        im = part[FRQ:, g * BLK:(g + 1) * BLK]
        work[g * FRQ:(g + 1) * FRQ, :BLK] = re * cos_t + im * sin_t
        work[g * FRQ:(g + 1) * FRQ, BLK:] = im * cos_t - re * sin_t
    return wide_dot(work[...], tab, 0)


def from_freq(re, im, rows, tab, trig):
    cos_t, sin_t = trig[:FRQ, :], trig[FRQ:, :]
    z = wide_dot(jnp.concatenate([re, im], axis=1), tab, 4 * BLK)
    pieces = []
    for g in range(GRP):
        zr = z[g * FRQ:(g + 1) * FRQ, :BLK]
        zi = z[g * FRQ:(g + 1) * FRQ, BLK:]
        pieces.append(jnp.concatenate([zr * cos_t - zi * sin_t, zr * sin_t + zi * cos_t], axis=0))
    hi, lo = split(jnp.concatenate(pieces, axis=1))
    last = tab[8 * BLK + 4 * FRQ:8 * BLK + 4 * FRQ + 2 * NBLK, :2 * FRQ]
    both = dot(last, hi)
    out = both[:NBLK] + both[NBLK:] + dot(last[:NBLK], lo)
    for g in range(GRP):
        rows[pl.ds(g, NBLK, stride=GRP), :] = out[:, g * BLK:(g + 1) * BLK]
    return rows[...]


def here(axis):
    return lax.axis_index(axis)


def flip(index, bit):
    return 1 - index if bit else index


def block_of(zl, j):
    return flip(here("yl"), j // 4) * 16 + zl * 4 + j % 4


def rows_at(index, count):
    return pl.ds(pl.multiple_of(index * count, count), count)


def to_channels(rows):
    return rows.T.astype(BF).reshape(NBLK, GRP, BLK)


def drop_kernel(cot, mask, keep, send, buf, cot_v, mask_v, sems):
    fetch((cot, mask), (cot_v, mask_v), sems)
    buf[...] = (cot_v[...].astype(F32) * mask_v[...].astype(F32) / keep_prob).astype(BF)
    for z in range(2):
        for out, core in ((keep, 0), (send, 1)):
            q = flip(here("zo"), z) * 2 + flip(here("c"), core)
            out[z] = buf[:, rows_at(q, BLK)]


def fetch(sources, places, sems):
    copies = [pltpu.make_async_copy(a, b, sems.at[n]) for n, (a, b) in enumerate(zip(sources, places))]
    for copy in copies:
        copy.start()
    for copy in copies:
        copy.wait()


def join_kernel(*refs):
    at = 0
    for ref in refs[:-1]:
        refs[-1][at:at + ref.shape[0]] = ref[...]
        at += ref.shape[0]


def pre_kernel(*refs):
    sources = refs[:4]
    both = refs[-6]
    fetch(sources, refs[-5:-1], refs[-1])
    taps, gate_in, value, gate_out = refs[-5:-1]
    for n, block in enumerate((taps[...], gate_in[...].astype(F32) * value[...].astype(F32), gate_out[...].astype(F32))):
        chan = to_channels(block)
        for p in range(NBLK):
            both[p, n * GRP:(n + 1) * GRP] = chan[OWNED[p]]


def conv_kernel(both, tab, trig, conv, taps_f, prod_f, m0, m1, m2, m3, rows, work, act):
    rows[...] = both[:, :GRP].astype(F32).reshape(NBLK * GRP, BLK)
    taps = to_freq(rows, work, tab, trig)
    taps_f[...] = taps
    rows[...] = both[:, GRP:2 * GRP].astype(F32).reshape(NBLK * GRP, BLK)
    prod = to_freq(rows, work, tab, trig)
    prod_f[...] = prod
    tr, ti, pr, pi = taps[:, :BLK], taps[:, BLK:], prod[:, :BLK], prod[:, BLK:]
    out = from_freq(tr * pr - ti * pi, tr * pi + ti * pr, rows, tab, trig).astype(BF)
    conv[...] = out.reshape(NBLK, GRP, BLK)
    act[...] = (both[:, 2 * GRP:].astype(F32).reshape(NBLK * GRP, BLK) * out.astype(F32)).astype(BF)
    for s, m in enumerate((m0, m1, m2, m3)):
        for j in range(8):
            m[:, j * BLK:(j + 1) * BLK] = act[rows_at(block_of((here("zl") + s) % NL, j), GRP), :]


def grad_kernel(g0, g1, g2, g3, both, conv, taps_f, prod_f, tab, trig, out_ref, rows, work):
    for s, g in enumerate((g0, g1, g2, g3)):
        for j in range(8):
            rows[rows_at(block_of((here("zl") + NL - s) % NL, j), GRP), :] = g[:, j * BLK:(j + 1) * BLK].astype(F32)
    mixed = rows[...]
    out_ref[:, 2 * GRP:] = (mixed * conv[...].astype(F32).reshape(NBLK * GRP, BLK)).astype(BF).reshape(NBLK, GRP, BLK)
    rows[...] = (mixed * both[:, 2 * GRP:].astype(F32).reshape(NBLK * GRP, BLK)).astype(BF).astype(F32)
    g = to_freq(rows, work, tab, trig)
    gr, gi = g[:, :BLK], g[:, BLK:]
    for n, other in enumerate((taps_f, prod_f)):
        r, i = other[:, :BLK], other[:, BLK:]
        out = from_freq(gr * r + gi * i, gi * r - gr * i, rows, tab, trig)
        if n:
            out = out * ROOT
        out_ref[:, n * GRP:(n + 1) * GRP] = out.astype(BF).reshape(NBLK, GRP, BLK)


def mm1_kernel(q0, q1, q2, q3, w0, w1, w2, cols, kept, sent, wall, full):
    for n, w in enumerate((w0, w1, w2[:BLK], w2[BLK:])):
        zl = flip(here("zl") // 2, n // 2) * 2 + flip(here("zl") % 2, n % 2)
        wall[rows_at((zl - here("x") + NL) % NL, BLK), :] = w[...]
    for r, q in enumerate((q0, q1, q2, q3)):
        for j in range(8):
            at = j // 4 * 4 + flip(here("zo"), j // 2 % 2) * 2 + flip(here("c"), j % 2)
            cols[rows_at(at, BLK), r * BLK:(r + 1) * BLK] = q[j * BLK:(j + 1) * BLK, :]
    a = cols[...]
    full[...] = lax.dot_general(wall[...], a, (((0,), (1,)), ((), ())), preferred_element_type=F32)
    for r in range(4):
        for out, core in ((kept, 0), (sent, 1)):
            e = flip(here("yh"), r // 2) * 4 + flip(here("zo"), r % 2) * 2 + flip(here("c"), core)
            out[r] = full[rows_at(e, 4 * GRP), :].astype(out.dtype)


def sum1_kernel(kept, got, own, s1, s2, s3):
    own[...] = kept[0] + got[0].astype(F32)
    for r, out in ((1, s1), (2, s2), (3, s3)):
        out[...] = (kept[r] + got[r].astype(F32)).astype(BF)


def sum2_kernel(own, g1, g2, g3, o0, o1, o2, o3, buf):
    buf[...] = (own[...] + g1[...].astype(F32) + g2[...].astype(F32) + g3[...].astype(F32)).astype(BF)
    for s, out in enumerate((o0, o1, o2, o3)):
        out[...] = buf[rows_at((here("zl") + s) % NL, GRP), :]


def mm2_kernel(cols, own, sib, o0, o1, o2, o3, mall, full):
    for core, src in enumerate((own, sib)):
        for r in range(4):
            for s in range(NL):
                b = flip(here("yh"), r // 2) * 16 + flip(here("zo"), r % 2) * 8 + flip(here("c"), core) * 4
                b = b + (here("zl") + NL - s) % NL
                mall[rows_at(b, GRP), :] = src[(r * NL + s) * GRP:(r * NL + s + 1) * GRP, :]
    full[...] = dot(mall[...], cols[...])
    base = here("zl") - here("x") + NL
    for s, out in enumerate((o0, o1, o2, o3)):
        out[...] = full[:, rows_at((base + s) % NL, BLK)].astype(out.dtype)


def sum3_kernel(o0, g1, g2, g3, out):
    total = o0[...] + g1[...].astype(F32) + g2[...].astype(F32) + g3[...].astype(F32)
    out[...] = total.T * ROOT


def post_kernel(outs, gate_in, value_in, ggo, ggi, gv, gf):
    def tokens(n):
        rows = [None] * NBLK
        for p in range(NBLK):
            rows[OWNED[p]] = outs[p, n * GRP:(n + 1) * GRP].astype(F32)
        return jnp.concatenate(rows, axis=0).T

    back = tokens(0)
    ggi[...] = (back * value_in[...].astype(F32)).astype(BF)
    gv[...] = (back * gate_in[...].astype(F32)).astype(BF)
    gf[...] = tokens(1)
    ggo[...] = tokens(2).astype(BF)


def call(kernel, outs, *args, scratch=(), far=0):
    scratch = [pltpu.SemaphoreType.DMA((s,)) if isinstance(s, int) else pltpu.VMEM(*s) for s in scratch]
    specs = [pl.BlockSpec(memory_space=pltpu.HBM if n < far else pltpu.VMEM) for n in range(len(args))]
    return pl.pallas_call(
        kernel, out_shape=outs, in_specs=specs, scratch_shapes=scratch,
        compiler_params=pltpu.CompilerParams(vmem_limit_bytes=LIMIT * 1024 * 1024),
    )(*args)


LIMIT = 32


def flips(value, axes, bits):
    size = NL if axes == ("zl",) else 2 ** len(axes)
    return lax.ppermute(value, axes, [(i, i ^ bits) for i in range(size)])


def turn(value, axis, shift):
    return lax.ppermute(value, axis, [(i, (i + shift) % NL) for i in range(NL)])


def crossing(far, z):
    return [(a * 4 + o * 2 + b, b * 4 + (o ^ z) * 2 + (a ^ far)) for a in range(2) for o in range(2) for b in range(2)]


def exchange(block):
    return lax.all_to_all(block, SEQ, split_axis=0, concat_axis=0, tiled=True)


def body(cotangent, keep_mask, gate_out, gate_in, value_in, filter_taps, out_weight):
    tab, trig = tables()
    small, rows, rows32 = SDS((GRP, TOK), BF), SDS((BLK, WID), BF), SDS((BLK, WID), F32)
    freq = SDS((GRP * FRQ, 2 * BLK), F32)
    conv_scratch = [((NBLK * GRP, BLK), F32), ((GRP * FRQ, 2 * BLK), F32)]
    low = flips(out_weight, ("zl",), 1)
    couple = call(join_kernel, SDS((2 * BLK, WID), BF), out_weight, low)
    weights = [out_weight, low, flips(couple, ("zl",), 2)]
    pairs = SDS((2, BLK, BLK), BF)
    keep, send = call(
        drop_kernel, (pairs, pairs), cotangent, keep_mask, far=2,
        scratch=[((BLK, WID), BF), ((BLK, WID), BF), ((BLK, WID), jnp.int32), 2],
    )
    got = flips(send, ("c",), 1)
    pair = jnp.stack([keep, got], axis=1).reshape(2, 2 * BLK, BLK)
    quad = call(
        join_kernel, SDS((TOK, BLK), BF),
        *[lax.ppermute(pair[z], ("yh", "zo", "yl"), crossing(far, z)) for far in range(2) for z in range(2)])
    pieces = [quad] + [turn(quad, "x", -r) for r in range(1, NL)]
    both = call(
        pre_kernel, SDS((NBLK, 3 * GRP, BLK), BF), filter_taps, gate_in, value_in, gate_out, quad, far=5,
        scratch=[((BLK, WID), F32)] + [((BLK, WID), BF)] * 3 + [4],
    )
    both = exchange(both)

    conv, taps_f, prod_f, *acts = call(
        conv_kernel, (SDS((NBLK, GRP, BLK), BF), freq, freq) + (small,) * 4, both, tab, trig,
        scratch=conv_scratch + [((NBLK * GRP, BLK), BF)],
    )
    cols, kept, sent = call(
        mm1_kernel, (SDS((TOK, WID), BF), SDS((4, 4 * GRP, TOK), F32), SDS((4, 4 * GRP, TOK), BF)),
        *pieces, *weights, scratch=[((WID, WID), BF), ((WID, TOK), F32)],
    )
    arrived = flips(sent, ("c",), 1)
    own, *parts = call(sum1_kernel, (SDS((4 * GRP, TOK), F32),) + (SDS((4 * GRP, TOK), BF),) * 3, kept, arrived)
    parts = [flips(v, ("yh", "zo"), b) for b, v in zip((1, 2, 3), parts)]
    grads = call(sum2_kernel, (small,) * 4, own, *parts, scratch=[((4 * GRP, TOK), BF)])
    grads = [grads[0]] + [turn(grads[s], "zl", s) for s in range(1, NL)]

    acts = [acts[0]] + [turn(acts[s], "zl", s) for s in range(1, NL)]
    act = call(join_kernel, SDS((4 * GRP, TOK), BF), *acts)
    group = call(join_kernel, SDS((WID // 2, TOK), BF), act, *[flips(act, ("yh", "zo"), b) for b in (1, 2, 3)])
    sibling = flips(group, ("c",), 1)
    tall = SDS((WID, BLK), BF)
    sums = call(
        mm2_kernel, (SDS((WID, BLK), F32), tall, tall, tall), cols, group, sibling,
        scratch=[((WID, TOK), BF), ((WID, WID), F32)],
    )
    sums = [sums[0]] + [turn(sums[s], "zl", s) for s in range(1, NL)]
    grad_weight = call(sum3_kernel, rows32, *sums)

    outs = call(
        grad_kernel, SDS((NBLK, 3 * GRP, BLK), BF), *grads, both, conv, taps_f, prod_f, tab, trig, scratch=conv_scratch)
    outs = exchange(outs)
    grad_gate_out, grad_gate_in, grad_value, grad_filter = call(
        post_kernel, (rows, rows, rows, rows32), outs, gate_in, value_in)
    return (grad_gate_out, grad_gate_in, grad_value, grad_filter, grad_weight)


def solution(mesh):
    fine = Mesh(mesh.devices.reshape(2, NL, 2, 2, 2, NL), AXES)
    spec = P(SEQ, CH)
    return jax.shard_map(body, mesh=fine, in_specs=(spec,) * 7, out_specs=(spec,) * 5, check_vma=False)
```

```python
import math

import jax
import jax.numpy as jnp
import ml_dtypes
import numpy as np
from jax import lax
from jax.experimental import pallas as pl
from jax.experimental.pallas import tpu as pltpu
from jax.sharding import Mesh, PartitionSpec as P

BF = jnp.bfloat16
F32 = jnp.float32
SDS = jax.ShapeDtypeStruct
keep_prob = 0.9
BLK = 128
NBLK = 32
GRP = 16
FRQ = 40
LEN = 2 * BLK * NBLK
WID = 4 * BLK
TOK = 8 * BLK
NL = 4
ROOT = 1.0 / math.sqrt(BLK * NBLK)
AXES = ("yh", "zl", "zo", "c", "yl", "x")
SEQ = ("yh", "zl", "zo", "c")
CH = ("yl", "x")
OWNED = [(p // 16) * 16 + (p // 2 % 2) * 8 + (p % 2) * 4 + (p // 4 % 4) for p in range(NBLK)]


def split_np(table):
    hi = table.astype(ml_dtypes.bfloat16)
    return hi, (table - hi.astype(np.float64)).astype(ml_dtypes.bfloat16)


def tables():
    f1 = np.arange(FRQ)[:, None]
    live = (f1 <= NBLK).astype(np.float64)
    k = np.arange(NBLK)[None, :]
    ang = 2 * np.pi * ((f1 * k) % (2 * NBLK)) / (2 * NBLK)
    first = np.concatenate([np.cos(ang) * live, -np.sin(ang) * live], 0)
    weight = np.where((f1 == 0) | (f1 == NBLK), 1.0, 2.0) * live / LEN
    last = np.concatenate([np.cos(ang) * weight, -np.sin(ang) * weight], 0).T
    s = np.arange(BLK)
    turns = 2 * np.pi * (f1 * s[None, :]) / LEN
    ang2 = 2 * np.pi * ((s[:, None] * s[None, :]) % BLK) / BLK
    c, d = np.cos(ang2), np.sin(ang2)
    fwd = np.block([[c, -d], [d, c]])
    inv = np.block([[c, d], [-d, c]])
    parts = [*split_np(fwd), *split_np(inv), *split_np(first), *split_np(last)]
    flat = np.zeros((sum(p.shape[0] for p in parts), 2 * BLK), ml_dtypes.bfloat16)
    at = 0
    for p in parts:
        flat[at:at + p.shape[0], :p.shape[1]] = p
        at += p.shape[0]
    return flat, np.concatenate([np.cos(turns), np.sin(turns)], 0).astype(np.float32)


def dot(a, b):
    return jnp.dot(a, b, preferred_element_type=F32)


def split(x):
    hi = x.astype(BF)
    return hi, (x - hi.astype(F32)).astype(BF)


def wide_dot(x, tab, at):
    hi, lo = split(x)
    hi_tab, lo_tab = tab[at:at + 2 * BLK, :], tab[at + 2 * BLK:at + 4 * BLK, :]
    return dot(hi, hi_tab) + dot(lo, hi_tab) + dot(hi, lo_tab)


def to_freq(rows, work, tab, trig):
    cos_t, sin_t = trig[:FRQ, :], trig[FRQ:, :]
    lanes = jnp.concatenate([rows[pl.ds(g, NBLK, stride=GRP), :] for g in range(GRP)], axis=1).astype(BF)
    both = dot(tab[8 * BLK:8 * BLK + 4 * FRQ, :NBLK], lanes)
    part = both[:2 * FRQ] + both[2 * FRQ:]
    for g in range(GRP):
        re = part[:FRQ, g * BLK:(g + 1) * BLK]
        im = part[FRQ:, g * BLK:(g + 1) * BLK]
        work[g * FRQ:(g + 1) * FRQ, :BLK] = re * cos_t + im * sin_t
        work[g * FRQ:(g + 1) * FRQ, BLK:] = im * cos_t - re * sin_t
    return wide_dot(work[...], tab, 0)


def from_freq(re, im, rows, tab, trig):
    cos_t, sin_t = trig[:FRQ, :], trig[FRQ:, :]
    z = wide_dot(jnp.concatenate([re, im], axis=1), tab, 4 * BLK)
    pieces = []
    for g in range(GRP):
        zr = z[g * FRQ:(g + 1) * FRQ, :BLK]
        zi = z[g * FRQ:(g + 1) * FRQ, BLK:]
        pieces.append(jnp.concatenate([zr * cos_t - zi * sin_t, zr * sin_t + zi * cos_t], axis=0))
    hi, lo = split(jnp.concatenate(pieces, axis=1))
    last = tab[8 * BLK + 4 * FRQ:8 * BLK + 4 * FRQ + 2 * NBLK, :2 * FRQ]
    both = dot(last, hi)
    out = both[:NBLK] + both[NBLK:] + dot(last[:NBLK], lo)
    for g in range(GRP):
        rows[pl.ds(g, NBLK, stride=GRP), :] = out[:, g * BLK:(g + 1) * BLK]
    return rows[...]


def here(axis):
    return lax.axis_index(axis)


def flip(index, bit):
    return 1 - index if bit else index


def block_of(zl, j):
    return flip(here("yl"), j // 4) * 16 + zl * 4 + j % 4


def rows_at(index, count):
    return pl.ds(pl.multiple_of(index * count, count), count)


def to_channels(rows):
    return rows.T.astype(BF).reshape(NBLK, GRP, BLK)


def drop_kernel(cot, mask, keep, send, buf, cot_v, mask_v, sems):
    fetch((cot, mask), (cot_v, mask_v), sems)
    buf[...] = (cot_v[...].astype(F32) * mask_v[...].astype(F32) / keep_prob).astype(BF)
    for z in range(2):
        for out, core in ((keep, 0), (send, 1)):
            q = flip(here("zo"), z) * 2 + flip(here("c"), core)
            out[z] = buf[:, rows_at(q, BLK)]


def fetch(sources, places, sems):
    copies = [pltpu.make_async_copy(a, b, sems.at[n]) for n, (a, b) in enumerate(zip(sources, places))]
    for copy in copies:
        copy.start()
    for copy in copies:
        copy.wait()


def join_kernel(*refs):
    at = 0
    for ref in refs[:-1]:
        refs[-1][at:at + ref.shape[0]] = ref[...]
        at += ref.shape[0]


def half_kernel(*refs):
    for n, ref in enumerate(refs[:-1]):
        refs[-1][n * GRP:(n + 1) * GRP] = ref[GRP:]


def pre_kernel(*refs):
    sources = refs[:4]
    both = refs[-6]
    fetch(sources, refs[-5:-1], refs[-1])
    taps, gate_in, value, gate_out = refs[-5:-1]
    for n, block in enumerate((taps[...], gate_in[...].astype(F32) * value[...].astype(F32), gate_out[...].astype(F32))):
        chan = to_channels(block)
        for p in range(NBLK):
            both[p, n * GRP:(n + 1) * GRP] = chan[OWNED[p]]


def conv_kernel(both, tab, trig, conv, taps_f, prod_f, m0, m1, m2, m3, rows, work, act):
    rows[...] = both[:, :GRP].astype(F32).reshape(NBLK * GRP, BLK)
    taps = to_freq(rows, work, tab, trig)
    taps_f[...] = taps
    rows[...] = both[:, GRP:2 * GRP].astype(F32).reshape(NBLK * GRP, BLK)
    prod = to_freq(rows, work, tab, trig)
    prod_f[...] = prod
    tr, ti, pr, pi = taps[:, :BLK], taps[:, BLK:], prod[:, :BLK], prod[:, BLK:]
    out = from_freq(tr * pr - ti * pi, tr * pi + ti * pr, rows, tab, trig).astype(BF)
    conv[...] = out.reshape(NBLK, GRP, BLK)
    act[...] = (both[:, 2 * GRP:].astype(F32).reshape(NBLK * GRP, BLK) * out.astype(F32)).astype(BF)
    for s, m in enumerate((m0, m1, m2, m3)):
        for j in range(8):
            m[:, j * BLK:(j + 1) * BLK] = act[rows_at(block_of((here("zl") + s) % NL, j), GRP), :]


def grad_kernel(g0, g1, g2, g3, both, conv, taps_f, prod_f, tab, trig, out_ref, rows, work):
    for s, g in enumerate((g0, g1, g2, g3)):
        for j in range(8):
            rows[rows_at(block_of((here("zl") + NL - s) % NL, j), GRP), :] = g[:GRP, j * BLK:(j + 1) * BLK].astype(F32)
    mixed = rows[...]
    out_ref[:, 2 * GRP:] = (mixed * conv[...].astype(F32).reshape(NBLK * GRP, BLK)).astype(BF).reshape(NBLK, GRP, BLK)
    rows[...] = (mixed * both[:, 2 * GRP:].astype(F32).reshape(NBLK * GRP, BLK)).astype(BF).astype(F32)
    g = to_freq(rows, work, tab, trig)
    gr, gi = g[:, :BLK], g[:, BLK:]
    for n, other in enumerate((taps_f, prod_f)):
        r, i = other[:, :BLK], other[:, BLK:]
        out = from_freq(gr * r + gi * i, gi * r - gr * i, rows, tab, trig)
        if n:
            out = out * ROOT
        out_ref[:, n * GRP:(n + 1) * GRP] = out.astype(BF).reshape(NBLK, GRP, BLK)


def mm1_kernel(q0, q1, q2, q3, w0, w1, w2, cols, kept, sent, wall, full):
    for n, w in enumerate((w0, w1, w2[:BLK], w2[BLK:])):
        zl = flip(here("zl") // 2, n // 2) * 2 + flip(here("zl") % 2, n % 2)
        wall[rows_at((zl - here("x") + NL) % NL, BLK), :] = w[...]
    for r, q in enumerate((q0, q1, q2, q3)):
        for j in range(8):
            at = j // 4 * 4 + flip(here("zo"), j // 2 % 2) * 2 + flip(here("c"), j % 2)
            cols[rows_at(at, BLK), r * BLK:(r + 1) * BLK] = q[j * BLK:(j + 1) * BLK, :]
    a = cols[...]
    full[...] = lax.dot_general(wall[...], a, (((0,), (1,)), ((), ())), preferred_element_type=F32)
    for r in range(4):
        for out, core in ((kept, 0), (sent, 1)):
            e = flip(here("yh"), r // 2) * 4 + flip(here("zo"), r % 2) * 2 + flip(here("c"), core)
            out[r] = full[rows_at(e, 4 * GRP), :].astype(out.dtype)


def sum1_kernel(kept, got, own, s1, s2, s3):
    own[...] = kept[0] + got[0].astype(F32)
    for r, out in ((1, s1), (2, s2), (3, s3)):
        out[...] = (kept[r] + got[r].astype(F32)).astype(BF)


def sum2_kernel(own, g1, g2, g3, m0, m1, m2, m3, o0, o1, o2, o3, buf):
    buf[...] = (own[...] + g1[...].astype(F32) + g2[...].astype(F32) + g3[...].astype(F32)).astype(BF)
    for s, (out, m) in enumerate(((o0, m0), (o1, m1), (o2, m2), (o3, m3))):
        out[:GRP] = buf[rows_at((here("zl") + s) % NL, GRP), :]
        out[GRP:] = m[...]


def mm2_kernel(cols, own, sib, o0, o1, o2, o3, mall, full):
    for core, src in enumerate((own, sib)):
        for r in range(4):
            for s in range(NL):
                b = flip(here("yh"), r // 2) * 16 + flip(here("zo"), r % 2) * 8 + flip(here("c"), core) * 4
                b = b + (here("zl") + NL - s) % NL
                mall[rows_at(b, GRP), :] = src[(r * NL + s) * GRP:(r * NL + s + 1) * GRP, :]
    full[...] = dot(mall[...], cols[...])
    base = here("zl") - here("x") + NL
    for s, out in enumerate((o0, o1, o2, o3)):
        out[...] = full[:, rows_at((base + s) % NL, BLK)].astype(out.dtype)


def sum3_kernel(o0, g1, g2, g3, out):
    total = o0[...] + g1[...].astype(F32) + g2[...].astype(F32) + g3[...].astype(F32)
    out[...] = total.T * ROOT


def post_kernel(outs, gate_in, value_in, ggo, ggi, gv, gf):
    def tokens(n):
        rows = [None] * NBLK
        for p in range(NBLK):
            rows[OWNED[p]] = outs[p, n * GRP:(n + 1) * GRP].astype(F32)
        return jnp.concatenate(rows, axis=0).T

    back = tokens(0)
    ggi[...] = (back * value_in[...].astype(F32)).astype(BF)
    gv[...] = (back * gate_in[...].astype(F32)).astype(BF)
    gf[...] = tokens(1)
    ggo[...] = tokens(2).astype(BF)


def call(kernel, outs, *args, scratch=(), far=0):
    scratch = [pltpu.SemaphoreType.DMA((s,)) if isinstance(s, int) else pltpu.VMEM(*s) for s in scratch]
    specs = [pl.BlockSpec(memory_space=pltpu.HBM if n < far else pltpu.VMEM) for n in range(len(args))]
    return pl.pallas_call(
        kernel, out_shape=outs, in_specs=specs, scratch_shapes=scratch,
        compiler_params=pltpu.CompilerParams(vmem_limit_bytes=LIMIT * 1024 * 1024),
    )(*args)


LIMIT = 44


def flips(value, axes, bits):
    size = NL if axes == ("zl",) else 2 ** len(axes)
    return lax.ppermute(value, axes, [(i, i ^ bits) for i in range(size)])


def turn(value, axis, shift):
    return lax.ppermute(value, axis, [(i, (i + shift) % NL) for i in range(NL)])


def crossing(far, z):
    return [(a * 4 + o * 2 + b, b * 4 + (o ^ z) * 2 + (a ^ far)) for a in range(2) for o in range(2) for b in range(2)]


def exchange(block):
    return lax.all_to_all(block, SEQ, split_axis=0, concat_axis=0, tiled=True)


def body(cotangent, keep_mask, gate_out, gate_in, value_in, filter_taps, out_weight):
    tab, trig = tables()
    small, rows, rows32 = SDS((GRP, TOK), BF), SDS((BLK, WID), BF), SDS((BLK, WID), F32)
    freq = SDS((GRP * FRQ, 2 * BLK), F32)
    conv_scratch = [((NBLK * GRP, BLK), F32), ((GRP * FRQ, 2 * BLK), F32)]
    low = flips(out_weight, ("zl",), 1)
    couple = call(join_kernel, SDS((2 * BLK, WID), BF), out_weight, low)
    weights = [out_weight, low, flips(couple, ("zl",), 2)]
    pairs = SDS((2, BLK, BLK), BF)
    keep, send = call(
        drop_kernel, (pairs, pairs), cotangent, keep_mask, far=2,
        scratch=[((BLK, WID), BF), ((BLK, WID), BF), ((BLK, WID), jnp.int32), 2],
    )
    got = flips(send, ("c",), 1)
    pair = jnp.stack([keep, got], axis=1).reshape(2, 2 * BLK, BLK)
    quad = call(
        join_kernel, SDS((TOK, BLK), BF),
        *[lax.ppermute(pair[z], ("yh", "zo", "yl"), crossing(far, z)) for far in range(2) for z in range(2)])
    pieces = [quad] + [turn(quad, "x", -r) for r in range(1, NL)]
    both = call(
        pre_kernel, SDS((NBLK, 3 * GRP, BLK), BF), filter_taps, gate_in, value_in, gate_out, quad, far=5,
        scratch=[((BLK, WID), F32)] + [((BLK, WID), BF)] * 3 + [4],
    )
    both = exchange(both)

    conv, taps_f, prod_f, *acts = call(
        conv_kernel, (SDS((NBLK, GRP, BLK), BF), freq, freq) + (small,) * 4, both, tab, trig,
        scratch=conv_scratch + [((NBLK * GRP, BLK), BF)],
    )
    cols, kept, sent = call(
        mm1_kernel, (SDS((TOK, WID), BF), SDS((4, 4 * GRP, TOK), F32), SDS((4, 4 * GRP, TOK), BF)),
        *pieces, *weights, scratch=[((WID, WID), BF), ((WID, TOK), F32)],
    )
    arrived = flips(sent, ("c",), 1)
    own, *parts = call(sum1_kernel, (SDS((4 * GRP, TOK), F32),) + (SDS((4 * GRP, TOK), BF),) * 3, kept, arrived)
    parts = [flips(v, ("yh", "zo"), b) for b, v in zip((1, 2, 3), parts)]
    grads = call(sum2_kernel, (SDS((2 * GRP, TOK), BF),) * 4, own, *parts, *acts, scratch=[((4 * GRP, TOK), BF)])
    grads = [grads[0]] + [turn(grads[s], "zl", s) for s in range(1, NL)]

    act = call(half_kernel, SDS((4 * GRP, TOK), BF), *grads)
    group = call(join_kernel, SDS((WID // 2, TOK), BF), act, *[flips(act, ("yh", "zo"), b) for b in (1, 2, 3)])
    sibling = flips(group, ("c",), 1)
    tall = SDS((WID, BLK), BF)
    sums = call(
        mm2_kernel, (SDS((WID, BLK), F32), tall, tall, tall), cols, group, sibling,
        scratch=[((WID, TOK), BF), ((WID, WID), F32)],
    )
    sums = [sums[0]] + [turn(sums[s], "zl", s) for s in range(1, NL)]
    grad_weight = call(sum3_kernel, rows32, *sums)

    outs = call(
        grad_kernel, SDS((NBLK, 3 * GRP, BLK), BF), *grads, both, conv, taps_f, prod_f, tab, trig, scratch=conv_scratch)
    outs = exchange(outs)
    grad_gate_out, grad_gate_in, grad_value, grad_filter = call(
        post_kernel, (rows, rows, rows, rows32), outs, gate_in, value_in)
    return (grad_gate_out, grad_gate_in, grad_value, grad_filter, grad_weight)


def solution(mesh):
    fine = Mesh(mesh.devices.reshape(2, NL, 2, 2, 2, NL), AXES)
    spec = P(SEQ, CH)
    return jax.shard_map(body, mesh=fine, in_specs=(spec,) * 7, out_specs=(spec,) * 5, check_vma=False)
```

```python
import math

import jax
import jax.numpy as jnp
import ml_dtypes
import numpy as np
from jax import lax
from jax.experimental import pallas as pl
from jax.experimental.pallas import tpu as pltpu
from jax.sharding import Mesh, PartitionSpec as P

BF = jnp.bfloat16
F32 = jnp.float32
SDS = jax.ShapeDtypeStruct
keep_prob = 0.9
BLK = 128
NBLK = 32
GRP = 16
FRQ = 40
LEN = 2 * BLK * NBLK
WID = 4 * BLK
TOK = 8 * BLK
NL = 4
ROOT = 1.0 / math.sqrt(BLK * NBLK)
AXES = ("yh", "zl", "zo", "c", "yl", "x")
SEQ = ("yh", "zl", "zo", "c")
CH = ("yl", "x")
OWNED = [(p // 16) * 16 + (p // 2 % 2) * 8 + (p % 2) * 4 + (p // 4 % 4) for p in range(NBLK)]


def split_np(table):
    hi = table.astype(ml_dtypes.bfloat16)
    return hi, (table - hi.astype(np.float64)).astype(ml_dtypes.bfloat16)


def tables():
    f1 = np.arange(FRQ)[:, None]
    live = (f1 <= NBLK).astype(np.float64)
    k = np.arange(NBLK)[None, :]
    ang = 2 * np.pi * ((f1 * k) % (2 * NBLK)) / (2 * NBLK)
    first = np.concatenate([np.cos(ang) * live, -np.sin(ang) * live], 0)
    weight = np.where((f1 == 0) | (f1 == NBLK), 1.0, 2.0) * live / LEN
    last = np.concatenate([np.cos(ang) * weight, -np.sin(ang) * weight], 0).T
    s = np.arange(BLK)
    turns = 2 * np.pi * (f1 * s[None, :]) / LEN
    ang2 = 2 * np.pi * ((s[:, None] * s[None, :]) % BLK) / BLK
    c, d = np.cos(ang2), np.sin(ang2)
    fwd = np.block([[c, -d], [d, c]])
    inv = np.block([[c, d], [-d, c]])
    parts = [*split_np(fwd), *split_np(inv), *split_np(first), *split_np(last)]
    flat = np.zeros((sum(p.shape[0] for p in parts), 2 * BLK), ml_dtypes.bfloat16)
    at = 0
    for p in parts:
        flat[at:at + p.shape[0], :p.shape[1]] = p
        at += p.shape[0]
    return flat, np.concatenate([np.cos(turns), np.sin(turns)], 0).astype(np.float32)


def dot(a, b):
    return jnp.dot(a, b, preferred_element_type=F32)


def split(x):
    hi = x.astype(BF)
    return hi, (x - hi.astype(F32)).astype(BF)


def wide_dot(x, tab, at):
    hi, lo = split(x)
    hi_tab, lo_tab = tab[at:at + 2 * BLK, :], tab[at + 2 * BLK:at + 4 * BLK, :]
    return dot(hi, hi_tab) + dot(lo, hi_tab) + dot(hi, lo_tab)


def to_freq(rows, work, tab, trig):
    cos_t, sin_t = trig[:FRQ, :], trig[FRQ:, :]
    lanes = jnp.concatenate([rows[pl.ds(g, NBLK, stride=GRP), :] for g in range(GRP)], axis=1).astype(BF)
    both = dot(tab[8 * BLK:8 * BLK + 4 * FRQ, :NBLK], lanes)
    part = both[:2 * FRQ] + both[2 * FRQ:]
    for g in range(GRP):
        re = part[:FRQ, g * BLK:(g + 1) * BLK]
        im = part[FRQ:, g * BLK:(g + 1) * BLK]
        work[g * FRQ:(g + 1) * FRQ, :BLK] = re * cos_t + im * sin_t
        work[g * FRQ:(g + 1) * FRQ, BLK:] = im * cos_t - re * sin_t
    return wide_dot(work[...], tab, 0)


def from_freq(re, im, rows, tab, trig):
    cos_t, sin_t = trig[:FRQ, :], trig[FRQ:, :]
    z = wide_dot(jnp.concatenate([re, im], axis=1), tab, 4 * BLK)
    pieces = []
    for g in range(GRP):
        zr = z[g * FRQ:(g + 1) * FRQ, :BLK]
        zi = z[g * FRQ:(g + 1) * FRQ, BLK:]
        pieces.append(jnp.concatenate([zr * cos_t - zi * sin_t, zr * sin_t + zi * cos_t], axis=0))
    hi, lo = split(jnp.concatenate(pieces, axis=1))
    last = tab[8 * BLK + 4 * FRQ:8 * BLK + 4 * FRQ + 2 * NBLK, :2 * FRQ]
    both = dot(last, hi)
    out = both[:NBLK] + both[NBLK:] + dot(last[:NBLK], lo)
    for g in range(GRP):
        rows[pl.ds(g, NBLK, stride=GRP), :] = out[:, g * BLK:(g + 1) * BLK]
    return rows[...]


def here(axis):
    return lax.axis_index(axis)


def flip(index, bit):
    return 1 - index if bit else index


def block_of(zl, j):
    return flip(here("yl"), j // 4) * 16 + zl * 4 + j % 4


def rows_at(index, count):
    return pl.ds(pl.multiple_of(index * count, count), count)


def to_channels(rows):
    return rows.T.astype(BF).reshape(NBLK, GRP, BLK)


def drop_kernel(cot, mask, keep, send, buf, cot_v, mask_v, sems):
    fetch((cot, mask), (cot_v, mask_v), sems)
    buf[...] = (cot_v[...].astype(F32) * mask_v[...].astype(F32) / keep_prob).astype(BF)
    for z in range(2):
        for out, core in ((keep, 0), (send, 1)):
            q = flip(here("zo"), z) * 2 + flip(here("c"), core)
            out[z] = buf[:, rows_at(q, BLK)]


def fetch(sources, places, sems):
    copies = [pltpu.make_async_copy(a, b, sems.at[n]) for n, (a, b) in enumerate(zip(sources, places))]
    for copy in copies:
        copy.start()
    for copy in copies:
        copy.wait()


def join_kernel(*refs):
    at = 0
    for ref in refs[:-1]:
        refs[-1][at:at + ref.shape[0]] = ref[...]
        at += ref.shape[0]


def half_kernel(*refs):
    for n, ref in enumerate(refs[:-1]):
        refs[-1][n * GRP:(n + 1) * GRP] = ref[GRP:]


def pre_kernel(*refs):
    sources = refs[:4]
    both = refs[-6]
    fetch(sources, refs[-5:-1], refs[-1])
    taps, gate_in, value, gate_out = refs[-5:-1]
    for n, block in enumerate((taps[...], gate_in[...].astype(F32) * value[...].astype(F32), gate_out[...].astype(F32))):
        chan = to_channels(block)
        for p in range(NBLK):
            both[p, n * GRP:(n + 1) * GRP] = chan[OWNED[p]]


def conv_kernel(both, tab, trig, conv, taps_f, prod_f, m0, m1, m2, m3, rows, work, act):
    rows[...] = both[:, :GRP].astype(F32).reshape(NBLK * GRP, BLK)
    taps = to_freq(rows, work, tab, trig)
    taps_f[...] = taps
    rows[...] = both[:, GRP:2 * GRP].astype(F32).reshape(NBLK * GRP, BLK)
    prod = to_freq(rows, work, tab, trig)
    prod_f[...] = prod
    tr, ti, pr, pi = taps[:, :BLK], taps[:, BLK:], prod[:, :BLK], prod[:, BLK:]
    out = from_freq(tr * pr - ti * pi, tr * pi + ti * pr, rows, tab, trig).astype(BF)
    conv[...] = out.reshape(NBLK, GRP, BLK)
    act[...] = (both[:, 2 * GRP:].astype(F32).reshape(NBLK * GRP, BLK) * out.astype(F32)).astype(BF)
    for s, m in enumerate((m0, m1, m2, m3)):
        for j in range(8):
            m[:, j * BLK:(j + 1) * BLK] = act[rows_at(block_of((here("zl") + s) % NL, j), GRP), :]


def grad_kernel(_, g0, g1, g2, g3, both, conv, taps_f, prod_f, tab, trig, out_ref, rows, work):
    for s, g in enumerate((g0, g1, g2, g3)):
        for j in range(8):
            rows[rows_at(block_of((here("zl") + NL - s) % NL, j), GRP), :] = g[:GRP, j * BLK:(j + 1) * BLK].astype(F32)
    mixed = rows[...]
    out_ref[:, 2 * GRP:] = (mixed * conv[...].astype(F32).reshape(NBLK * GRP, BLK)).astype(BF).reshape(NBLK, GRP, BLK)
    rows[...] = (mixed * both[:, 2 * GRP:].astype(F32).reshape(NBLK * GRP, BLK)).astype(BF).astype(F32)
    g = to_freq(rows, work, tab, trig)
    gr, gi = g[:, :BLK], g[:, BLK:]
    for n, other in enumerate((taps_f, prod_f)):
        r, i = other[:, :BLK], other[:, BLK:]
        out = from_freq(gr * r + gi * i, gi * r - gr * i, rows, tab, trig)
        if n:
            out = out * ROOT
        out_ref[:, n * GRP:(n + 1) * GRP] = out.astype(BF).reshape(NBLK, GRP, BLK)


def mm1_kernel(q0, q1, q2, q3, w0, w1, w2, cols, kept, sent, wall, full):
    for n, w in enumerate((w0, w1, w2[:BLK], w2[BLK:])):
        zl = flip(here("zl") // 2, n // 2) * 2 + flip(here("zl") % 2, n % 2)
        wall[rows_at((zl - here("x") + NL) % NL, BLK), :] = w[...]
    for r, q in enumerate((q0, q1, q2, q3)):
        for j in range(8):
            at = j // 4 * 4 + flip(here("zo"), j // 2 % 2) * 2 + flip(here("c"), j % 2)
            cols[rows_at(at, BLK), r * BLK:(r + 1) * BLK] = q[j * BLK:(j + 1) * BLK, :]
    a = cols[...]
    full[...] = lax.dot_general(wall[...], a, (((0,), (1,)), ((), ())), preferred_element_type=F32)
    for r in range(4):
        for out, core in ((kept, 0), (sent, 1)):
            e = flip(here("yh"), r // 2) * 4 + flip(here("zo"), r % 2) * 2 + flip(here("c"), core)
            out[r] = full[rows_at(e, 4 * GRP), :].astype(out.dtype)


def sum1_kernel(kept, got, own, s1, s2, s3):
    own[...] = kept[0] + got[0].astype(F32)
    for r, out in ((1, s1), (2, s2), (3, s3)):
        out[...] = (kept[r] + got[r].astype(F32)).astype(BF)


def sum2_kernel(own, g1, g2, g3, m0, m1, m2, m3, o0, o1, o2, o3, buf):
    buf[...] = (own[...] + g1[...].astype(F32) + g2[...].astype(F32) + g3[...].astype(F32)).astype(BF)
    for s, (out, m) in enumerate(((o0, m0), (o1, m1), (o2, m2), (o3, m3))):
        out[:GRP] = buf[rows_at((here("zl") + s) % NL, GRP), :]
        out[GRP:] = m[...]


def mm2_kernel(cols, *refs):
    o0, o1, o2, o3, mall, full = refs[8:]
    for core, src in enumerate((refs[:4], refs[4:8])):
        for r in range(4):
            for s in range(NL):
                b = flip(here("yh"), r // 2) * 16 + flip(here("zo"), r % 2) * 8 + flip(here("c"), core) * 4
                b = b + (here("zl") + NL - s) % NL
                mall[rows_at(b, GRP), :] = src[r][s * GRP:(s + 1) * GRP, :]
    full[...] = dot(mall[...], cols[...])
    base = here("zl") - here("x") + NL
    for s, out in enumerate((o0, o1, o2, o3)):
        out[...] = full[:, rows_at((base + s) % NL, BLK)].astype(out.dtype)


def sum3_kernel(o0, g1, g2, g3, out):
    total = o0[...] + g1[...].astype(F32) + g2[...].astype(F32) + g3[...].astype(F32)
    out[...] = total.T * ROOT


def post_kernel(outs, gate_in, value_in, ggo, ggi, gv, gf):
    def tokens(n):
        rows = [None] * NBLK
        for p in range(NBLK):
            rows[OWNED[p]] = outs[p, n * GRP:(n + 1) * GRP].astype(F32)
        return jnp.concatenate(rows, axis=0).T

    back = tokens(0)
    ggi[...] = (back * value_in[...].astype(F32)).astype(BF)
    gv[...] = (back * gate_in[...].astype(F32)).astype(BF)
    gf[...] = tokens(1)
    ggo[...] = tokens(2).astype(BF)


def call(kernel, outs, *args, scratch=(), far=0):
    scratch = [pltpu.SemaphoreType.DMA((s,)) if isinstance(s, int) else pltpu.VMEM(*s) for s in scratch]
    specs = [pl.BlockSpec(memory_space=pltpu.HBM if n < far else pltpu.VMEM) for n in range(len(args))]
    return pl.pallas_call(
        kernel, out_shape=outs, in_specs=specs, scratch_shapes=scratch,
        compiler_params=pltpu.CompilerParams(vmem_limit_bytes=LIMIT * 1024 * 1024),
    )(*args)


LIMIT = 44


def flips(value, axes, bits):
    size = NL if axes == ("zl",) else 2 ** len(axes)
    return lax.ppermute(value, axes, [(i, i ^ bits) for i in range(size)])


def turn(value, axis, shift):
    return lax.ppermute(value, axis, [(i, (i + shift) % NL) for i in range(NL)])


def crossing(far, z):
    return [(a * 4 + o * 2 + b, b * 4 + (o ^ z) * 2 + (a ^ far)) for a in range(2) for o in range(2) for b in range(2)]


def exchange(block):
    return lax.all_to_all(block, SEQ, split_axis=0, concat_axis=0, tiled=True)


def body(cotangent, keep_mask, gate_out, gate_in, value_in, filter_taps, out_weight):
    tab, trig = tables()
    small, rows, rows32 = SDS((GRP, TOK), BF), SDS((BLK, WID), BF), SDS((BLK, WID), F32)
    freq = SDS((GRP * FRQ, 2 * BLK), F32)
    conv_scratch = [((NBLK * GRP, BLK), F32), ((GRP * FRQ, 2 * BLK), F32)]
    low = flips(out_weight, ("zl",), 1)
    couple = call(join_kernel, SDS((2 * BLK, WID), BF), out_weight, low)
    weights = [out_weight, low, flips(couple, ("zl",), 2)]
    pairs = SDS((2, BLK, BLK), BF)
    keep, send = call(
        drop_kernel, (pairs, pairs), cotangent, keep_mask, far=2,
        scratch=[((BLK, WID), BF), ((BLK, WID), BF), ((BLK, WID), jnp.int32), 2],
    )
    got = flips(send, ("c",), 1)
    pair = jnp.stack([keep, got], axis=1).reshape(2, 2 * BLK, BLK)
    quad = call(
        join_kernel, SDS((TOK, BLK), BF),
        *[lax.ppermute(pair[z], ("yh", "zo", "yl"), crossing(far, z)) for far in range(2) for z in range(2)])
    pieces = [quad] + [turn(quad, "x", -r) for r in range(1, NL)]
    both = call(
        pre_kernel, SDS((NBLK, 3 * GRP, BLK), BF), filter_taps, gate_in, value_in, gate_out, quad, far=5,
        scratch=[((BLK, WID), F32)] + [((BLK, WID), BF)] * 3 + [4],
    )
    both = exchange(both)

    conv, taps_f, prod_f, *acts = call(
        conv_kernel, (SDS((NBLK, GRP, BLK), BF), freq, freq) + (small,) * 4, both, tab, trig,
        scratch=conv_scratch + [((NBLK * GRP, BLK), BF)],
    )
    cols, kept, sent = call(
        mm1_kernel, (SDS((TOK, WID), BF), SDS((4, 4 * GRP, TOK), F32), SDS((4, 4 * GRP, TOK), BF)),
        *pieces, *weights, scratch=[((WID, WID), BF), ((WID, TOK), F32)],
    )
    arrived = flips(sent, ("c",), 1)
    own, *parts = call(sum1_kernel, (SDS((4 * GRP, TOK), F32),) + (SDS((4 * GRP, TOK), BF),) * 3, kept, arrived)
    parts = [flips(v, ("yh", "zo"), b) for b, v in zip((1, 2, 3), parts)]
    grads = call(sum2_kernel, (SDS((2 * GRP, TOK), BF),) * 4, own, *parts, *acts, scratch=[((4 * GRP, TOK), BF)])
    grads = [grads[0]] + [turn(grads[s], "zl", s) for s in range(1, NL)]

    act = call(half_kernel, SDS((4 * GRP, TOK), BF), *grads)
    group = [act] + [flips(act, ("yh", "zo"), b) for b in (1, 2, 3)]
    sibling = [flips(v, ("c",), 1) for v in group]
    tall = SDS((WID, BLK), BF)
    sums = call(
        mm2_kernel, (SDS((WID, BLK), F32), tall, tall, tall), cols, *group, *sibling,
        scratch=[((WID, TOK), BF), ((WID, WID), F32)],
    )
    sums = [sums[0]] + [turn(sums[s], "zl", s) for s in range(1, NL)]
    grad_weight = call(sum3_kernel, rows32, *sums)

    outs = call(
        grad_kernel, SDS((NBLK, 3 * GRP, BLK), BF), group[1], *grads, both, conv, taps_f, prod_f, tab, trig, scratch=conv_scratch, far=1)
    outs = exchange(outs)
    grad_gate_out, grad_gate_in, grad_value, grad_filter = call(
        post_kernel, (rows, rows, rows, rows32), outs, gate_in, value_in)
    return (grad_gate_out, grad_gate_in, grad_value, grad_filter, grad_weight)


def solution(mesh):
    fine = Mesh(mesh.devices.reshape(2, NL, 2, 2, 2, NL), AXES)
    spec = P(SEQ, CH)
    return jax.shard_map(body, mesh=fine, in_specs=(spec,) * 7, out_specs=(spec,) * 5, check_vma=False)
```
